256 devices in a mesh: turn: 32 (over z_hi, x, core), line: 8 (over z_lo, y).
Axes of the slice: x: 4, y: 4, z: 8 (z_hi: 4, z_lo: 2; z = z_hi * 2 + z_lo), core: 2. Of those that a mesh axis runs over, the one named last changes fastest.
Arguments:
- flop_cards: int32 [2, 3], replicated, may hold values from 0 to 51, as said below
- turn_cards: int32 [2, 32], P(None, 'turn'), may hold values from 0 to 51, as said below
- river_cards: int32 [2, 32, 8], P(None, 'turn'), may hold values from 0 to 51, as said below
- ranks: int32 [2, 32, 8, 1326], P(None, 'turn'), may hold values from 0 to 7461
- flop_reach: float32 [2, 1326], replicated, may hold values from 0.05 to 1
- turn_policy: bfloat16 [2, 32, 8, 4, 1326], P(None, 'turn', 'line'), may hold values from 0.049804688 to 1
- river_policy: bfloat16 [2, 32, 8, 8, 4, 4, 4, 1326], P(None, 'turn', None, 'line'), may hold values from 0.049804688 to 1
- stake: float32 [8, 4, 4, 4], P('line'), may hold values from 0.5 to 4
Outputs:
- turn_values: float32 [2, 32, 1326], P(None, 'turn')
- flop_value: float32 [2, 1326], replicated
The draws below stay inside these ranges and needn't reach their ends.
Inputs may be any that keep to these rules, and one draw needn't show every extreme that they name: `turn_cards`: for each flop, the flop cards and the turn cards are distinct cards of 0 to 51. `river_cards`: under each turn card the river cards are distinct and differ from that turn card and the flop cards. `flop_cards`: distinct from the turn and river cards of the same flop; the first flop holds card 52 - 1.
All inputs are finite; a program needn't handle non-finite values.
Results may differ from the reference program's by a relative error of at most 0.0003.
Values may be sent and summed in bfloat16 or wider, within the bound.
No kernel may reach another device: no remote copies, remote signals or barrier semaphores. Data moves between devices by JAX's collectives and lax.ppermute only.
A program may use at most 64 MiB of HBM per device.

```python
import math
import jax
import jax.numpy as jnp
import numpy as np
from jax import lax

CARDS = 52
H = 1326
FLOPS = 2
TURNS = 32
RIVERS = 8
A_T = 8
B_T = 4
A_R = 4
B_R = 4


def deal_cards(key):
    shuffles = jax.vmap(lambda sub: jax.random.permutation(sub, CARDS))(jax.random.split(jax.random.fold_in(key, 11), FLOPS))
    first = shuffles[0]
    top_place = jnp.argmax((first == CARDS - 1).astype(jnp.int32)).astype(jnp.int32)
    slot = jax.random.randint(jax.random.fold_in(key, 13), (), 0, 3).astype(jnp.int32)
    moved = first[slot]
    first = first.at[top_place].set(moved).at[slot].set(CARDS - 1)
    shuffles = shuffles.at[0].set(first)
    offsets = jax.vmap(lambda sub: jax.random.permutation(sub, CARDS - 4))(jax.random.split(jax.random.fold_in(key, 12), FLOPS * TURNS))
    offsets = offsets[:, :RIVERS].reshape(FLOPS, TURNS, RIVERS)
    remaining = shuffles[:, 3:]
    positions = (jnp.arange(TURNS, dtype=jnp.int32)[None, :, None] + 1 + offsets) % (CARDS - 3)
    spread = jnp.broadcast_to(remaining[:, None, :], (FLOPS, TURNS, CARDS - 3))
    rivers = jnp.take_along_axis(spread, positions, axis=2)
    return (shuffles[:, :3].astype(jnp.int32), remaining[:, :TURNS].astype(jnp.int32), rivers.astype(jnp.int32))


def draw_flop_cards(key, part):
    return deal_cards(key)[0]


def draw_turn_cards(key, part):
    return deal_cards(key)[1]


def draw_river_cards(key, part):
    return deal_cards(key)[2]


def touch_ends(entries, stream_key, least, largest):
    index_at = [jax.random.randint(jax.random.fold_in(stream_key, axis), (), 0, length) for axis, length in enumerate(entries.shape)]
    widest = entries.shape.index(max(entries.shape))
    next_to = index_at[:widest] + [(index_at[widest] + 1) % entries.shape[widest]] + index_at[widest + 1:]
    return entries.at[tuple(index_at)].set(least).at[tuple(next_to)].set(largest)


def block_scale(own_key, extent, shards, low, largest):
    loudness = 1.0
    for axis_at, blocks in shards:
        draws = jax.random.uniform(jax.random.fold_in(jax.random.fold_in(own_key, 6), axis_at), (blocks,), jnp.float32, low / len(shards), largest / len(shards))
        loudness = loudness * jnp.repeat(jnp.exp(draws), extent[axis_at] // blocks).reshape((-1,) + (1,) * (len(extent) - 1 - axis_at))
    return loudness


def setup_inputs(seed: int = 0) -> dict:
    keys = jax.random.split(jax.random.key(seed), 9)
    return {
        "flop_cards": draw_flop_cards(jax.random.fold_in(keys[8], 71), 0),
        "turn_cards": draw_turn_cards(jax.random.fold_in(keys[8], 71), 0),
        "river_cards": draw_river_cards(jax.random.fold_in(keys[8], 71), 0),
        "ranks": touch_ends(jax.random.randint(keys[3], (FLOPS, TURNS, RIVERS, H), 0, 7462), jax.random.fold_in(keys[3], 1), 0, 7461).astype(jnp.int32),
        "flop_reach": jnp.clip(jnp.exp(jax.random.uniform(keys[4], (FLOPS, H), jnp.float32, math.log(0.05), math.log(1.0))), 0.05, 1.0),
        "turn_policy": jnp.clip(jnp.exp(math.log(1.0) - 2.9996462 * jax.random.uniform(keys[5], (FLOPS, TURNS, A_T, B_T, H), jnp.float32) ** block_scale(keys[5], (FLOPS, TURNS, A_T, B_T, H), ((1, 32), (2, 8)), -0.2, 0.2)), 0.049804688, 1.0).astype(jnp.bfloat16),
        "river_policy": jnp.clip(jnp.exp(math.log(1.0) - 2.9996462 * jax.random.uniform(keys[6], (FLOPS, TURNS, RIVERS, A_T, B_T, A_R, B_R, H), jnp.float32) ** block_scale(keys[6], (FLOPS, TURNS, RIVERS, A_T, B_T, A_R, B_R, H), ((1, 32), (3, 8)), -0.2, 0.2)), 0.049804688, 1.0).astype(jnp.bfloat16),
        "stake": jnp.clip(jnp.exp(math.log(4.0) - 2.0794415 * jax.random.uniform(keys[7], (A_T, B_T, A_R, B_R), jnp.float32) ** block_scale(keys[7], (A_T, B_T, A_R, B_R), ((0, 8),), -0.2, 0.2)), 0.5, 4.0),
    }


def hand_cards():
    lower_card, upper_card = np.triu_indices(CARDS, 1)
    return jnp.asarray(lower_card.astype(np.int32)), jnp.asarray(upper_card.astype(np.int32))


def unblocked_by(cards, lower_card, upper_card):
    column = cards[..., :, None]
    struck = (lower_card == column) | (upper_card == column)
    return 1.0 - jnp.any(struck, axis=-2).astype(jnp.float32)


def card_conflict(lower_card, upper_card):
    return ((lower_card[:, None] == lower_card[None, :]) | (lower_card[:, None] == upper_card[None, :])
            | (upper_card[:, None] == lower_card[None, :]) | (upper_card[:, None] == upper_card[None, :]))


def showdown(strength, line_reach, shared_card):
    verdict = jnp.sign(strength[None, :] - strength[:, None]).astype(jnp.float32)
    payoff = jnp.where(shared_card, 0.0, verdict).astype(jnp.bfloat16)
    return jnp.dot(line_reach, payoff, preferred_element_type=jnp.float32)


def reference(flop_cards, turn_cards, river_cards, ranks, flop_reach, turn_policy, river_policy, stake):
    lower_card, upper_card = hand_cards()
    hand_count = lower_card.shape[0]
    shared_card = card_conflict(lower_card, upper_card)
    flop_clear = unblocked_by(flop_cards, lower_card, upper_card)
    opening = flop_reach * flop_clear
    turn_weights = turn_policy.astype(jnp.float32)
    turn_prob = turn_weights / jnp.sum(turn_weights, axis=3, keepdims=True)

    def one_turn(position):
        flop_index = position // TURNS
        turn_index = position % TURNS
        turn_clear = flop_clear[flop_index] * unblocked_by(turn_cards[flop_index, turn_index][None], lower_card, upper_card)
        turn_part = turn_prob[flop_index, turn_index]

        def one_river(river_index):
            river_card = river_cards[flop_index, turn_index, river_index]
            unblocked = turn_clear * unblocked_by(river_card[None], lower_card, upper_card)
            river_weights = river_policy[flop_index, turn_index, river_index].astype(jnp.float32)
            river_prob = river_weights / jnp.sum(river_weights, axis=3, keepdims=True)
            reach = (opening[flop_index] * unblocked)[None, None, None, None, :] * turn_part[:, :, None, None, :] * river_prob
            reach = reach.astype(jnp.bfloat16).reshape(-1, hand_count)
            leaves = showdown(ranks[flop_index, turn_index, river_index], reach, shared_card)
            leaves = leaves.reshape(river_prob.shape) * stake[..., None]
            values = jnp.max(jnp.sum(leaves, axis=3), axis=2)
            return jnp.sum(values, axis=1) * unblocked[None, :]

        totals = jnp.sum(lax.map(one_river, jnp.arange(RIVERS, dtype=jnp.int32)), axis=0) / RIVERS
        return jnp.max(totals, axis=0)

    turn_values = lax.map(one_turn, jnp.arange(FLOPS * TURNS, dtype=jnp.int32)).reshape(FLOPS, TURNS, hand_count)
    flop_value = jnp.sum(turn_values, axis=1) / TURNS
    return turn_values, flop_value
```

```python
import functools

import jax
import jax.numpy as jnp
import numpy as np
from jax import lax
from jax.experimental import pallas as pl
from jax.experimental.pallas import tpu as pltpu
from jax.sharding import Mesh
from jax.sharding import PartitionSpec as P

CARDS = 52
LANES = 128
F8 = jnp.float8_e4m3fn
F32 = jnp.float32
BF16 = jnp.bfloat16


def hand_cards():
    lower_card, upper_card = np.triu_indices(CARDS, 1)
    return lower_card.astype(np.int32), upper_card.astype(np.int32)


def padded(hands):
    return -(-hands // LANES) * LANES


def holds_rows(hands):
    lower_card, upper_card = hand_cards()
    width = padded(hands)
    holds = np.zeros((64, width), np.float32)
    holds[lower_card, np.arange(hands)] = 1.0
    holds[upper_card, np.arange(hands)] = 1.0
    return holds


def ordered(ranks):
    octave = ranks >> 7
    low = jnp.left_shift(1, jnp.minimum(octave, 29)).astype(F32)
    high = jnp.left_shift(1, jnp.maximum(octave - 29, 0)).astype(F32)
    return ((ranks & 127) + 128).astype(F32) * low * high


def board_kernel(
    flop_cards, turn_cards, river_cards, holds_ref, cards_ref, ranks_ref, flop_reach_ref, turn_ref, stake_ref, river_ref,
    out_ref, mask_ref, strength_ref, column_ref, payoff_ref, *, rivers, hands,
):
    width = padded(hands)
    board = pl.program_id(0)
    flop = board // rivers
    river = lax.rem(board, rivers)
    tiles = [(at, min(256, width - at)) for at in range(0, width, 256)]

    @pl.when(board == 0)
    def _():
        holds = holds_ref[...]
        for at, size in tiles:
            shared = lax.dot_general(holds, holds[:, at:at + size], (((0,), (0,)), ((), ())), preferred_element_type=F32)
            mask_ref[:, at:at + size] = (1.0 - jnp.minimum(shared, 1.0)).astype(BF16)
        strength = ordered(ranks_ref[...])
        pad = jnp.zeros((strength.shape[0], width - hands), F32)
        strength = jnp.concatenate([strength, pad], axis=1)
        for row in range(strength.shape[0]):
            strength_ref[row] = strength[row:row + 1]
        for at in range(0, width, LANES):
            column_ref[at:at + LANES, :] = strength[:, at:at + LANES].T

    lower, upper = cards_ref[0:1, :], cards_ref[1:2, :]

    def clear_of(card):
        return jnp.where((lower == card) | (upper == card), 0.0, 1.0)

    flop_clear = clear_of(flop_cards[flop, 0]) * clear_of(flop_cards[flop, 1]) * clear_of(flop_cards[flop, 2])
    unblocked = flop_clear * clear_of(turn_cards[flop, 0]) * clear_of(river_cards[flop, river])
    opening = flop_reach_ref[flop] * unblocked
    turn = turn_ref[flop].astype(F32)
    turn_prob = turn / jnp.sum(turn, axis=0, keepdims=True)
    weights = river_ref[0].astype(F32)
    total = jnp.sum(weights, axis=1)
    staked = jnp.sum(weights * stake_ref[...], axis=1)
    share = staked / total
    lines = share.reshape(4, 4, hands) * (opening * turn_prob)[:, None, :]
    lines = lines.reshape(16, hands)
    lines = jnp.concatenate([lines, jnp.zeros((16, width - hands), F32)], axis=1)
    parts = lines.astype(BF16)

    columns = column_ref[...]
    lane = lax.broadcasted_iota(jnp.int32, columns.shape, 1)
    column = jnp.sum(jnp.where(lane == board, columns, 0.0), axis=1, keepdims=True)
    column = jnp.broadcast_to(column, (width, LANES)).astype(BF16)
    leaves = []
    for at, size in tiles:
        for part in range(at, at + size, LANES):
            row = strength_ref[board, :, part:part + LANES].astype(BF16)
            mask = mask_ref[:, part:part + LANES]
            sign = jnp.minimum(jnp.maximum(row - column, -mask), mask)
            payoff_ref[:, part:part + LANES] = sign.astype(F8)
        product = jnp.dot(parts, payoff_ref[:, at:at + size], preferred_element_type=F32)
        leaves.append(product)
    leaves = jnp.concatenate(leaves, axis=1)[:, :hands].reshape(4, 4, hands)
    value = jnp.sum(jnp.max(leaves, axis=1), axis=0, keepdims=True) * unblocked

    @pl.when(river == 0)
    def _():
        out_ref[flop] = jnp.zeros((1, hands), F32)

    out_ref[flop] += value


def board_values(flop_cards, turn_cards, river_cards, ranks, flop_reach, turn_policy, river_policy, stake):
    flops, rivers, hands = ranks.shape
    boards = flops * rivers
    width = padded(hands)
    smem = pl.BlockSpec(memory_space=pltpu.SMEM)
    whole = lambda *shape: pl.BlockSpec(shape, lambda b: (0,) * len(shape))
    cards = jnp.asarray(np.stack(hand_cards()))
    return pl.pallas_call(
        functools.partial(board_kernel, rivers=rivers, hands=hands),
        grid=(boards,),
        in_specs=[
            smem, smem, smem,
            whole(64, width), whole(2, hands), whole(boards, hands), whole(flops, 1, hands), whole(flops, 4, hands),
            whole(16, 4, 1),
            pl.BlockSpec((1, 16, 4, hands), lambda b: (b, 0, 0, 0)),
        ],
        out_specs=whole(flops, 1, hands),
        out_shape=jax.ShapeDtypeStruct((flops, 1, hands), F32),
        scratch_shapes=[
            pltpu.VMEM((width, width), BF16),
            pltpu.VMEM((boards, 1, width), F32),
            pltpu.VMEM((width, boards), F32),
            pltpu.VMEM((width, width), F8),
        ],
        compiler_params=pltpu.CompilerParams(vmem_limit_bytes=48 * 2**20),
        name="boards",
    )(
        flop_cards, turn_cards, river_cards, jnp.asarray(holds_rows(hands), BF16), cards, ranks.reshape(boards, hands),
        flop_reach[:, None], turn_policy, stake.reshape(16, 4, 1), river_policy.reshape(boards, 16, 4, hands),
    )


def swap(values, axis, size, flip, combine):
    return combine(values, lax.ppermute(values, axis, [(i, i ^ flip) for i in range(size)]))


def local(flop_cards, turn_cards, river_cards, ranks, flop_reach, turn_policy, river_policy, stake):
    rivers = river_cards.shape[2]
    totals = board_values(
        flop_cards, turn_cards, river_cards[:, 0], ranks[:, 0], flop_reach, turn_policy[:, 0, 0], river_policy[:, 0, :, 0], stake[0]
    )
    values = totals / rivers
    values = swap(values, "z_lo", 2, 1, jnp.maximum)
    values = swap(values, "y", 4, 1, jnp.maximum)
    values = swap(values, "y", 4, 3, jnp.maximum)
    total = swap(values, "core", 2, 1, jnp.add)
    total = swap(total, "x", 4, 1, jnp.add)
    total = swap(total, "x", 4, 3, jnp.add)
    total = swap(total, "z_hi", 4, 1, jnp.add)
    total = swap(total, "z_hi", 4, 3, jnp.add)
    return values, total[:, 0] / 32


def solution(mesh):
    fine = Mesh(mesh.devices.reshape(4, 4, 2, 2, 4), ("z_hi", "x", "core", "z_lo", "y"))
    turn, line = ("z_hi", "x", "core"), ("z_lo", "y")
    in_specs = (
        P(),
        P(None, turn),
        P(None, turn, None),
        P(None, turn, None, None),
        P(),
        P(None, turn, line, None, None),
        P(None, turn, None, line, None, None, None, None),
        P(line, None, None, None),
    )
    out_specs = (P(None, turn, None), P())
    return jax.shard_map(local, mesh=fine, in_specs=in_specs, out_specs=out_specs, check_vma=False)
```

```python
import functools

import jax
import jax.numpy as jnp
from jax import lax
from jax.experimental import pallas as pl
from jax.experimental.pallas import tpu as pltpu
from jax.sharding import Mesh
from jax.sharding import PartitionSpec as P

CARDS = 52
LANES = 128
F8 = jnp.float8_e4m3fn
F32 = jnp.float32
BF16 = jnp.bfloat16
GROUP = 4
DEPTH = 256


def padded(hands):
    return -(-hands // LANES) * LANES


def hand_cards(width):
    hand = lax.broadcasted_iota(jnp.int32, (1, width), 1)

    def first_of(lower):
        return (lower * (2 * CARDS - 1 - lower)) >> 1

    root = jnp.sqrt(jnp.maximum(((2 * CARDS - 1) ** 2 - 8 * hand).astype(F32), 0.0))
    lower = ((2 * CARDS - 1 - root) * 0.5).astype(jnp.int32)
    lower = lower + (first_of(lower + 1) <= hand).astype(jnp.int32)
    lower = lower - (first_of(lower) > hand).astype(jnp.int32)
    return lower, hand - first_of(lower) + lower + 1


def ordered(ranks):
    octave = ranks >> 7
    low = jnp.left_shift(1, jnp.minimum(octave, 29)).astype(F32)
    high = jnp.left_shift(1, jnp.maximum(octave - 29, 0)).astype(F32)
    return ((ranks & 127) + 128).astype(F32) * low * high


def board_kernel(
    flop_cards_in, turn_cards_in, river_cards_in, ranks_in, flop_reach_in, turn_in, stake_in, river_in, out_ref,
    flop_cards, turn_cards, river_cards, ranks_ref, flop_reach_ref, turn_ref, stake_ref, river_ref,
    free_ref, minus_ref, rows_ref, columns_ref, clear_ref, entry_ref, payoff_ref, leaves_ref, sems, river_sems, *, hands,
):
    flops, rivers = river_cards.shape
    boards = flops * rivers
    width = padded(hands)
    group = GROUP
    tiles = [(at, min(256, width - at)) for at in range(0, width, 256)]
    pairs = [
        (flop_cards_in, flop_cards), (turn_cards_in, turn_cards), (river_cards_in, river_cards), (ranks_in, ranks_ref),
        (flop_reach_in, flop_reach_ref), (turn_in, turn_ref), (stake_in, stake_ref),
    ]
    copies = [pltpu.make_async_copy(source, target, sems.at[i]) for i, (source, target) in enumerate(pairs)]
    for copy in copies:
        copy.start()

    def river_copy(board):
        return pltpu.make_async_copy(river_in.at[board], river_ref.at[board], river_sems.at[board])

    for board in range(boards):
        river_copy(board).start()

    lower, upper = hand_cards(width)
    card = lax.broadcasted_iota(jnp.int32, (64, width), 0)
    holds = jnp.where((card == lower) | (card == upper), 1.0, 0.0).astype(BF16)
    for at, size in tiles:
        shared = lax.dot_general(holds, holds[:, at:at + size], (((0,), (0,)), ((), ())), preferred_element_type=F32)
        free = jnp.maximum(1.0 - shared, 0.0).astype(BF16)
        free_ref[:, at:at + size] = free
        minus_ref[:, at:at + size] = -free
    for copy in copies:
        copy.wait()
    strength = ordered(ranks_ref[...])
    strength = jnp.concatenate([strength, jnp.zeros((boards, width - hands), F32)], axis=1)
    for row in range(boards):
        rows_ref[row] = jnp.broadcast_to(strength[row:row + 1], (16, width)).astype(BF16)
    for at in range(0, width, LANES):
        for first in range(0, boards, group):
            columns_ref[first // group, at:at + LANES, :] = strength[first:first + group, at:at + LANES].T

    def clear_of(card):
        return jnp.where((lower == card) | (upper == card), 0.0, 1.0)

    def widen(values):
        return jnp.concatenate([values, jnp.zeros((values.shape[0], width - hands), F32)], axis=1)

    for flop in range(flops):
        clear = clear_of(turn_cards[flop])
        for i in range(3):
            clear = clear * clear_of(flop_cards[flop, i])
        clear_ref[flop] = clear
        turn = turn_ref[flop].astype(F32)
        turn_prob = turn / jnp.sum(turn, axis=0, keepdims=True)
        entry_ref[flop] = widen(flop_reach_ref[flop:flop + 1, :] * turn_prob) * clear

    stake16 = stake_ref[...].reshape(16, 4)
    lane = lax.broadcasted_iota(jnp.int32, (16, 64), 1)
    own = (lane >> 2) == lax.broadcasted_iota(jnp.int32, (16, 64), 0)
    pots = jnp.zeros((16, 64), F32)
    for reply in range(4):
        pots = jnp.where((lane & 3) == reply, stake16[:, reply:reply + 1], pots)
    pots = jnp.where(own, pots, 0.0)
    coarse = pots.astype(BF16)
    spread = jnp.concatenate([own.astype(BF16), coarse, (pots - coarse.astype(F32)).astype(BF16)], axis=0)

    def one_group(at_group, acc):
        first = at_group * group
        flop = first // rivers
        lines, clears = [], []
        for i in range(group):
            river_copy(first + i).wait()
        for i in range(group):
            sums = jnp.dot(spread, river_ref[first + i].reshape(64, hands), preferred_element_type=F32)
            share = (sums[16:32] + sums[32:48]) / sums[:16]
            clear = clear_of(river_cards[flop, lax.rem(first + i, rivers)])
            reach = share.reshape(4, 4, hands) * (entry_ref[flop] * clear)[:, None, :hands]
            lines.append(widen(reach.reshape(16, hands)).astype(BF16))
            clears.append(clear)
        for chunk in range(0, width, DEPTH):
            stop = min(chunk + DEPTH, width)
            for down in range(chunk, stop, 32):
                column = [
                    jnp.broadcast_to(columns_ref[at_group, down:down + 32, i:i + 1], (32, LANES)).astype(BF16)
                    for i in range(group)
                ]
                for at in range(0, width, LANES):
                    free = free_ref[down:down + 32, at:at + LANES]
                    minus = minus_ref[down:down + 32, at:at + LANES]
                    for i in range(group):
                        row = rows_ref[first + i, :, at:at + LANES]
                        gap = jnp.concatenate([row, row], axis=0) - column[i]
                        payoff_ref[i, down:down + 32, at:at + LANES] = jnp.minimum(jnp.maximum(gap, minus), free).astype(F8)
            for i in range(group):
                product = jnp.dot(lines[i][:, chunk:stop], payoff_ref[i, chunk:stop, :], preferred_element_type=F32)
                if chunk == 0:
                    leaves_ref[i] = product
                else:
                    leaves_ref[i] += product
        value = jnp.zeros((1, width), F32)
        for i in range(group):
            best = jnp.max(leaves_ref[i].reshape(4, 4, width), axis=1)
            value = value + jnp.sum(best, axis=0, keepdims=True) * clears[i]
        return acc + value

    groups = rivers // group
    for flop in range(flops):
        value = lax.fori_loop(flop * groups, (flop + 1) * groups, one_group, jnp.zeros((1, width), F32))
        out_ref[flop:flop + 1, :] = (value * clear_ref[flop] * (1 / rivers))[:, :hands]


def board_values(flop_cards, turn_cards, river_cards, ranks, flop_reach, turn_policy, river_policy, stake):
    flops, rivers, hands = ranks.shape
    boards = flops * rivers
    width = padded(hands)
    args = (
        flop_cards, turn_cards, river_cards, ranks.reshape(boards, hands), flop_reach, turn_policy, stake,
        river_policy.reshape(boards, 16, 4, hands),
    )
    held = [(pltpu.SMEM if i < 3 else pltpu.VMEM)(a.shape, a.dtype) for i, a in enumerate(args)]
    return pl.pallas_call(
        functools.partial(board_kernel, hands=hands),
        in_specs=[pl.BlockSpec(memory_space=pl.ANY)] * len(args),
        out_specs=pl.BlockSpec(memory_space=pltpu.VMEM),
        out_shape=jax.ShapeDtypeStruct((flops, hands), F32),
        scratch_shapes=held + [
            pltpu.VMEM((width, width), BF16),
            pltpu.VMEM((width, width), BF16),
            pltpu.VMEM((boards, 16, width), BF16),
            pltpu.VMEM((boards // GROUP, width, GROUP), F32),
            pltpu.VMEM((flops, 1, width), F32),
            pltpu.VMEM((flops, 4, width), F32),
            pltpu.VMEM((GROUP, width, width), F8),
            pltpu.VMEM((GROUP, 16, width), F32),
            pltpu.SemaphoreType.DMA((len(args) - 1,)),
            pltpu.SemaphoreType.DMA((boards,)),
        ],
        compiler_params=pltpu.CompilerParams(vmem_limit_bytes=56 * 2**20),
        name="boards",
    )(*args)


def swap(values, axis, size, flip, combine):
    return combine(values, lax.ppermute(values, axis, [(i, i ^ flip) for i in range(size)]))


def local(flop_cards, turn_cards, river_cards, ranks, flop_reach, turn_policy, river_policy, stake):
    values = board_values(
        flop_cards, turn_cards[:, 0], river_cards[:, 0], ranks[:, 0], flop_reach, turn_policy[:, 0, 0],
        river_policy[:, 0, :, 0], stake[0]
    )
    values = swap(values, "z_lo", 2, 1, jnp.maximum)
    values = swap(values, "y", 4, 1, jnp.maximum)
    values = swap(values, "y", 4, 3, jnp.maximum)
    total = swap(values, "core", 2, 1, jnp.add)
    total = swap(total, "x", 4, 1, jnp.add)
    total = swap(total, "x", 4, 3, jnp.add)
    total = swap(total, "z_hi", 4, 1, jnp.add)
    total = swap(total, "z_hi", 4, 3, jnp.add)
    return values[:, None, :], total / 32


def solution(mesh):
    fine = Mesh(mesh.devices.reshape(4, 4, 2, 2, 4), ("z_hi", "x", "core", "z_lo", "y"))
    turn, line = ("z_hi", "x", "core"), ("z_lo", "y")
    in_specs = (
        P(),
        P(None, turn),
        P(None, turn, None),
        P(None, turn, None, None),
        P(),
        P(None, turn, line, None, None),
        P(None, turn, None, line, None, None, None, None),
        P(line, None, None, None),
    )
    out_specs = (P(None, turn, None), P())
    return jax.shard_map(local, mesh=fine, in_specs=in_specs, out_specs=out_specs, check_vma=False)
```

```python
import functools

import jax
import jax.numpy as jnp
from jax import lax
from jax.experimental import pallas as pl
from jax.experimental.pallas import tpu as pltpu
from jax.sharding import Mesh
from jax.sharding import PartitionSpec as P

CARDS = 52
LANES = 128
F8 = jnp.float8_e4m3fn
F32 = jnp.float32
BF16 = jnp.bfloat16
GROUP = 4
DEPTH = 256


def padded(hands):
    return -(-hands // LANES) * LANES


def hand_cards(width):
    hand = lax.broadcasted_iota(jnp.int32, (1, width), 1)

    def first_of(lower):
        return (lower * (2 * CARDS - 1 - lower)) >> 1

    root = jnp.sqrt(jnp.maximum(((2 * CARDS - 1) ** 2 - 8 * hand).astype(F32), 0.0))
    lower = ((2 * CARDS - 1 - root) * 0.5).astype(jnp.int32)
    lower = lower + (first_of(lower + 1) <= hand).astype(jnp.int32)
    lower = lower - (first_of(lower) > hand).astype(jnp.int32)
    return lower, hand - first_of(lower) + lower + 1


def ordered(ranks):
    octave = ranks >> 7
    low = jnp.left_shift(1, jnp.minimum(octave, 29)).astype(F32)
    high = jnp.left_shift(1, jnp.maximum(octave - 29, 0)).astype(F32)
    return ((ranks & 127) + 128).astype(F32) * low * high


def board_kernel(
    flop_cards_in, turn_cards_in, river_cards_in, ranks_in, flop_reach_in, turn_in, stake_in, river_in, out_ref,
    flop_cards, turn_cards, river_cards, ranks_ref, flop_reach_ref, turn_ref, stake_ref, river_ref,
    free_ref, rows_ref, columns_ref, wide_ref, clear_ref, entry_ref, payoff_ref, leaves_ref, sems, river_sems, *, hands,
):
    flops, rivers = river_cards.shape
    boards = flops * rivers
    width = padded(hands)
    group = GROUP
    tiles = [(at, min(256, width - at)) for at in range(0, width, 256)]
    pairs = [
        (flop_cards_in, flop_cards), (turn_cards_in, turn_cards), (river_cards_in, river_cards), (ranks_in, ranks_ref),
        (flop_reach_in, flop_reach_ref), (turn_in, turn_ref), (stake_in, stake_ref),
    ]
    copies = [pltpu.make_async_copy(source, target, sems.at[i]) for i, (source, target) in enumerate(pairs)]
    for copy in copies:
        copy.start()

    def river_copy(board):
        return pltpu.make_async_copy(river_in.at[board], river_ref.at[board], river_sems.at[board])

    for board in range(boards):
        river_copy(board).start()

    lower, upper = hand_cards(width)
    card = lax.broadcasted_iota(jnp.int32, (64, width), 0)
    holds = jnp.where((card == lower) | (card == upper), 1.0, 0.0).astype(BF16)
    for at, size in tiles:
        shared = lax.dot_general(holds, holds[:, at:at + size], (((0,), (0,)), ((), ())), preferred_element_type=F32)
        free = jnp.maximum(1.0 - shared, 0.0).astype(BF16)
        free_ref[:, at:at + size] = free
    for copy in copies:
        copy.wait()
    strength = ordered(ranks_ref[...])
    strength = jnp.concatenate([strength, jnp.zeros((boards, width - hands), F32)], axis=1)
    for row in range(boards):
        rows_ref[row] = jnp.broadcast_to(strength[row:row + 1], (16, width)).astype(BF16)
    for at in range(0, width, LANES):
        columns_ref[at:at + LANES, :] = strength[:, at:at + LANES].T.astype(BF16)
    for board in range(0, boards, 2):
        lane = lax.broadcasted_iota(jnp.int32, (boards, 2 * LANES), 1) // LANES + board
        pick = (lane == lax.broadcasted_iota(jnp.int32, lane.shape, 0)).astype(BF16)
        both = jnp.dot(columns_ref[...], pick, preferred_element_type=F32).astype(BF16)
        wide_ref[board] = both[:, :LANES]
        wide_ref[board + 1] = both[:, LANES:]

    def clear_of(card):
        return jnp.where((lower == card) | (upper == card), 0.0, 1.0)

    def widen(values):
        return jnp.concatenate([values, jnp.zeros((values.shape[0], width - hands), F32)], axis=1)

    for flop in range(flops):
        clear = clear_of(turn_cards[flop])
        for i in range(3):
            clear = clear * clear_of(flop_cards[flop, i])
        clear_ref[flop] = clear
        turn = turn_ref[flop].astype(F32)
        turn_prob = turn / jnp.sum(turn, axis=0, keepdims=True)
        entry_ref[flop] = widen(flop_reach_ref[flop:flop + 1, :] * turn_prob) * clear

    stake16 = stake_ref[...].reshape(16, 4)
    lane = lax.broadcasted_iota(jnp.int32, (16, 64), 1)
    own = (lane >> 2) == lax.broadcasted_iota(jnp.int32, (16, 64), 0)
    pots = jnp.zeros((16, 64), F32)
    for reply in range(4):
        pots = jnp.where((lane & 3) == reply, stake16[:, reply:reply + 1], pots)
    pots = jnp.where(own, pots, 0.0)
    coarse = pots.astype(BF16)
    spread = jnp.concatenate([own.astype(BF16), coarse, (pots - coarse.astype(F32)).astype(BF16)], axis=0)

    def one_group(at_group, acc):
        first = at_group * group
        flop = first // rivers
        lines, clears = [], []
        for i in range(group):
            river_copy(first + i).wait()
        for i in range(group):
            sums = jnp.dot(spread, river_ref[first + i].reshape(64, hands), preferred_element_type=F32)
            share = (sums[16:32] + sums[32:48]) / sums[:16]
            clear = clear_of(river_cards[flop, lax.rem(first + i, rivers)])
            reach = share.reshape(4, 4, hands) * (entry_ref[flop] * clear)[:, None, :hands]
            lines.append(widen(reach.reshape(16, hands)).astype(BF16))
            clears.append(clear)
        for chunk in range(0, width, DEPTH):
            stop = min(chunk + DEPTH, width)
            for down in range(chunk, stop, 32):
                column = [wide_ref[first + i, down:down + 32, :] for i in range(group)]
                for at in range(0, width, LANES):
                    free = free_ref[down:down + 32, at:at + LANES]
                    for i in range(group):
                        row = rows_ref[first + i, :, at:at + LANES]
                        gap = jnp.concatenate([row, row], axis=0) - column[i]
                        sign = jnp.minimum(jnp.maximum(gap, -1.0), 1.0) * free
                        payoff_ref[i, down:down + 32, at:at + LANES] = sign.astype(F8)
            for i in range(group):
                product = jnp.dot(lines[i][:, chunk:stop], payoff_ref[i, chunk:stop, :], preferred_element_type=F32)
                if chunk == 0:
                    leaves_ref[i] = product
                else:
                    leaves_ref[i] += product
        value = jnp.zeros((1, width), F32)
        for i in range(group):
            best = jnp.max(leaves_ref[i].reshape(4, 4, width), axis=1)
            value = value + jnp.sum(best, axis=0, keepdims=True) * clears[i]
        return acc + value

    groups = rivers // group
    for flop in range(flops):
        value = lax.fori_loop(flop * groups, (flop + 1) * groups, one_group, jnp.zeros((1, width), F32))
        out_ref[flop:flop + 1, :] = (value * clear_ref[flop] * (1 / rivers))[:, :hands]


def board_values(flop_cards, turn_cards, river_cards, ranks, flop_reach, turn_policy, river_policy, stake):
    flops, rivers, hands = ranks.shape
    boards = flops * rivers
    width = padded(hands)
    args = (
        flop_cards, turn_cards, river_cards, ranks.reshape(boards, hands), flop_reach, turn_policy, stake,
        river_policy.reshape(boards, 16, 4, hands),
    )
    held = [(pltpu.SMEM if i < 3 else pltpu.VMEM)(a.shape, a.dtype) for i, a in enumerate(args)]
    return pl.pallas_call(
        functools.partial(board_kernel, hands=hands),
        in_specs=[pl.BlockSpec(memory_space=pl.ANY)] * len(args),
        out_specs=pl.BlockSpec(memory_space=pltpu.VMEM),
        out_shape=pltpu.VMEM((flops, hands), F32),
        scratch_shapes=held + [
            pltpu.VMEM((width, width), BF16),
            pltpu.VMEM((boards, 16, width), BF16),
            pltpu.VMEM((width, boards), BF16),
            pltpu.VMEM((boards, width, LANES), BF16),
            pltpu.VMEM((flops, 1, width), F32),
            pltpu.VMEM((flops, 4, width), F32),
            pltpu.VMEM((GROUP, width, width), F8),
            pltpu.VMEM((GROUP, 16, width), F32),
            pltpu.SemaphoreType.DMA((len(args) - 1,)),
            pltpu.SemaphoreType.DMA((boards,)),
        ],
        compiler_params=pltpu.CompilerParams(vmem_limit_bytes=56 * 2**20),
        name="boards",
    )(*args)


def swaps(values, axis, size, flips, combine):
    parts = [lax.ppermute(values, axis, [(i, i ^ flip) for i in range(size)]) for flip in flips]
    return functools.reduce(combine, parts, values)


def local(flop_cards, turn_cards, river_cards, ranks, flop_reach, turn_policy, river_policy, stake):
    values = board_values(
        flop_cards, turn_cards[:, 0], river_cards[:, 0], ranks[:, 0], flop_reach, turn_policy[:, 0, 0],
        river_policy[:, 0, :, 0], stake[0]
    )
    line = ("z_lo", "y")
    copies = jnp.broadcast_to(values[None], (lax.axis_size(line),) + values.shape)
    values = jnp.max(lax.all_to_all(copies, line, 0, 0), axis=0)
    total = swaps(values, "core", 2, (1,), jnp.add)
    total = swaps(total, "x", 4, (1, 3, 2), jnp.add)
    total = swaps(total, "z_hi", 4, (1,), jnp.add)
    total = swaps(total, "z_hi", 4, (3,), jnp.add)
    return values[:, None, :], total / 32


def solution(mesh):
    fine = Mesh(mesh.devices.reshape(4, 4, 2, 2, 4), ("z_hi", "x", "core", "z_lo", "y"))
    turn, line = ("z_hi", "x", "core"), ("z_lo", "y")
    in_specs = (
        P(),
        P(None, turn),
        P(None, turn, None),
        P(None, turn, None, None),
        P(),
        P(None, turn, line, None, None),
        P(None, turn, None, line, None, None, None, None),
        P(line, None, None, None),
    )
    out_specs = (P(None, turn, None), P())
    return jax.shard_map(local, mesh=fine, in_specs=in_specs, out_specs=out_specs, check_vma=False)
```

```python
import functools

import jax
import jax.numpy as jnp
from jax import lax
from jax.experimental import pallas as pl
from jax.experimental.pallas import tpu as pltpu
from jax.sharding import Mesh
from jax.sharding import PartitionSpec as P

CARDS = 52
LANES = 128
F8 = jnp.float8_e4m3fn
F32 = jnp.float32
BF16 = jnp.bfloat16
GROUP = 4
DEPTH = 256
SPLIT = 8


def padded(hands):
    return -(-hands // LANES) * LANES


def hand_cards(width):
    hand = lax.broadcasted_iota(jnp.int32, (1, width), 1)

    def first_of(lower):
        return (lower * (2 * CARDS - 1 - lower)) >> 1

    root = jnp.sqrt(jnp.maximum(((2 * CARDS - 1) ** 2 - 8 * hand).astype(F32), 0.0))
    lower = ((2 * CARDS - 1 - root) * 0.5).astype(jnp.int32)
    lower = lower + (first_of(lower + 1) <= hand).astype(jnp.int32)
    lower = lower - (first_of(lower) > hand).astype(jnp.int32)
    return lower, hand - first_of(lower) + lower + 1


def ordered(ranks):
    octave = ranks >> 7
    low = jnp.left_shift(1, jnp.minimum(octave, 29)).astype(F32)
    high = jnp.left_shift(1, jnp.maximum(octave - 29, 0)).astype(F32)
    return ((ranks & 127) + 128).astype(F32) * low * high


def board_kernel(
    flop_cards_in, turn_cards_in, river_cards_in, ranks_in, flop_reach_in, turn_in, stake_in, river_in, out_ref,
    flop_cards, turn_cards, river_cards, ranks_ref, flop_reach_ref, turn_ref, stake_ref, river_ref,
    free_ref, rows_ref, columns_ref, wide_ref, clear_ref, entry_ref, payoff_ref, leaves_ref, sems, river_sems, *, hands,
):
    flops, rivers = river_cards.shape
    boards = flops * rivers
    width = padded(hands)
    depth = -(-hands // 64) * 64
    group = GROUP
    tiles = [(at, min(256, width - at)) for at in range(0, width, 256)]
    pairs = [
        (flop_cards_in, flop_cards), (turn_cards_in, turn_cards), (river_cards_in, river_cards), (ranks_in, ranks_ref),
        (flop_reach_in, flop_reach_ref), (turn_in, turn_ref), (stake_in, stake_ref),
    ]
    copies = [pltpu.make_async_copy(source, target, sems.at[i]) for i, (source, target) in enumerate(pairs)]
    for copy in copies:
        copy.start()

    def river_copy(board):
        return pltpu.make_async_copy(river_in.at[board], river_ref.at[board], river_sems.at[board])

    for board in range(boards):
        river_copy(board).start()

    lower, upper = hand_cards(width)
    card = lax.broadcasted_iota(jnp.int32, (64, width), 0)
    holds = jnp.where((card == lower) | (card == upper), 1.0, 0.0).astype(BF16)
    for at, size in tiles:
        shared = lax.dot_general(holds, holds[:, at:at + size], (((0,), (0,)), ((), ())), preferred_element_type=F32)
        free = jnp.maximum(1.0 - shared, 0.0).astype(BF16)
        free_ref[:, at:at + size] = free
    for copy in copies:
        copy.wait()
    strength = ordered(ranks_ref[...])
    strength = jnp.concatenate([strength, jnp.zeros((boards, width - hands), F32)], axis=1)
    for row in range(boards):
        rows_ref[row] = jnp.broadcast_to(strength[row:row + 1], (16, width)).astype(BF16)
    for at in range(0, width, LANES):
        columns_ref[at:at + LANES, :] = strength[:, at:at + LANES].T.astype(BF16)
    half = SPLIT
    for board in range(half, boards):
        for down in range(0, depth, 64):
            column = columns_ref[down:down + 64, board:board + 1].astype(F32)
            wide_ref[board, down:down + 64, :] = jnp.broadcast_to(column, (64, LANES)).astype(BF16)
    for board in range(0, half, 2):
        lane = lax.broadcasted_iota(jnp.int32, (boards, 2 * LANES), 1) // LANES + board
        pick = (lane == lax.broadcasted_iota(jnp.int32, lane.shape, 0)).astype(BF16)
        both = jnp.dot(columns_ref[:depth, :], pick, preferred_element_type=F32).astype(BF16)
        wide_ref[board, :depth] = both[:, :LANES]
        wide_ref[board + 1, :depth] = both[:, LANES:]

    def clear_of(card):
        return jnp.where((lower == card) | (upper == card), 0.0, 1.0)

    def widen(values):
        return jnp.concatenate([values, jnp.zeros((values.shape[0], width - hands), F32)], axis=1)

    for flop in range(flops):
        clear = clear_of(turn_cards[flop])
        for i in range(3):
            clear = clear * clear_of(flop_cards[flop, i])
        clear_ref[flop] = clear
        turn = turn_ref[flop].astype(F32)
        turn_prob = turn / jnp.sum(turn, axis=0, keepdims=True)
        entry_ref[flop] = widen(flop_reach_ref[flop:flop + 1, :] * turn_prob) * clear

    stake16 = stake_ref[...].reshape(16, 4)
    lane = lax.broadcasted_iota(jnp.int32, (16, 64), 1)
    own = (lane >> 2) == lax.broadcasted_iota(jnp.int32, (16, 64), 0)
    pots = jnp.zeros((16, 64), F32)
    for reply in range(4):
        pots = jnp.where((lane & 3) == reply, stake16[:, reply:reply + 1], pots)
    pots = jnp.where(own, pots, 0.0)
    coarse = pots.astype(BF16)
    spread = jnp.concatenate([own.astype(BF16), coarse, (pots - coarse.astype(F32)).astype(BF16)], axis=0)

    def one_group(at_group, acc):
        first = at_group * group
        flop = first // rivers
        lines, clears = [], []
        for i in range(group):
            river_copy(first + i).wait()
        for i in range(group):
            sums = jnp.dot(spread, river_ref[first + i].reshape(64, hands), preferred_element_type=F32)
            share = (sums[16:32] + sums[32:48]) / sums[:16]
            clear = clear_of(river_cards[flop, lax.rem(first + i, rivers)])
            reach = share.reshape(4, 4, hands) * (entry_ref[flop] * clear)[:, None, :hands]
            lines.append(widen(reach.reshape(16, hands)).astype(BF16))
            clears.append(clear)
        for chunk in range(0, depth, DEPTH):
            stop = min(chunk + DEPTH, depth)
            for down in range(chunk, stop, 32):
                column = [wide_ref[first + i, down:down + 32, :] for i in range(group)]
                for at in range(0, width, LANES):
                    free = free_ref[down:down + 32, at:at + LANES]
                    for i in range(group):
                        row = rows_ref[first + i, :, at:at + LANES]
                        gap = jnp.concatenate([row, row], axis=0) - column[i]
                        sign = jnp.minimum(jnp.maximum(gap, -1.0), 1.0) * free
                        payoff_ref[i, down:down + 32, at:at + LANES] = sign.astype(F8)
            for i in range(group):
                product = jnp.dot(lines[i][:, chunk:stop], payoff_ref[i, chunk:stop, :], preferred_element_type=F32)
                if chunk == 0:
                    leaves_ref[i] = product
                else:
                    leaves_ref[i] += product
        value = jnp.zeros((1, width), F32)
        for i in range(group):
            best = jnp.max(leaves_ref[i].reshape(4, 4, width), axis=1)
            value = value + jnp.sum(best, axis=0, keepdims=True) * clears[i]
        return acc + value

    groups = rivers // group
    for flop in range(flops):
        value = lax.fori_loop(flop * groups, (flop + 1) * groups, one_group, jnp.zeros((1, width), F32))
        out_ref[flop:flop + 1, :] = (value * clear_ref[flop] * (1 / rivers))[:, :hands]


def board_values(flop_cards, turn_cards, river_cards, ranks, flop_reach, turn_policy, river_policy, stake):
    flops, rivers, hands = ranks.shape
    boards = flops * rivers
    width = padded(hands)
    args = (
        flop_cards, turn_cards, river_cards, ranks.reshape(boards, hands), flop_reach, turn_policy, stake,
        river_policy.reshape(boards, 16, 4, hands),
    )
    held = [(pltpu.SMEM if i < 3 else pltpu.VMEM)(a.shape, a.dtype) for i, a in enumerate(args)]
    return pl.pallas_call(
        functools.partial(board_kernel, hands=hands),
        in_specs=[pl.BlockSpec(memory_space=pl.ANY)] * len(args),
        out_specs=pl.BlockSpec(memory_space=pltpu.VMEM),
        out_shape=pltpu.VMEM((flops, hands), F32),
        scratch_shapes=held + [
            pltpu.VMEM((width, width), BF16),
            pltpu.VMEM((boards, 16, width), BF16),
            pltpu.VMEM((width, boards), BF16),
            pltpu.VMEM((boards, width, LANES), BF16),
            pltpu.VMEM((flops, 1, width), F32),
            pltpu.VMEM((flops, 4, width), F32),
            pltpu.VMEM((GROUP, width, width), F8),
            pltpu.VMEM((GROUP, 16, width), F32),
            pltpu.SemaphoreType.DMA((len(args) - 1,)),
            pltpu.SemaphoreType.DMA((boards,)),
        ],
        compiler_params=pltpu.CompilerParams(vmem_limit_bytes=56 * 2**20),
        name="boards",
    )(*args)


def swaps(values, axis, size, flips, combine):
    parts = [lax.ppermute(values, axis, [(i, i ^ flip) for i in range(size)]) for flip in flips]
    return functools.reduce(combine, parts, values)


def local(flop_cards, turn_cards, river_cards, ranks, flop_reach, turn_policy, river_policy, stake):
    values = board_values(
        flop_cards, turn_cards[:, 0], river_cards[:, 0], ranks[:, 0], flop_reach, turn_policy[:, 0, 0],
        river_policy[:, 0, :, 0], stake[0]
    )
    line = ("z_lo", "y")
    copies = jnp.broadcast_to(values[None], (lax.axis_size(line),) + values.shape)
    values = jnp.max(lax.all_to_all(copies, line, 0, 0), axis=0)
    total = swaps(values, "core", 2, (1,), jnp.add)
    pairs = [(2 * i + core, 2 * (i ^ flip) + core) for i in range(4) for core, flip in ((0, 1), (1, 3))]
    near = lax.ppermute(total, ("x", "core"), pairs)
    total = swaps(total, "x", 4, (2,), jnp.add) + near + lax.ppermute(near, "core", [(0, 1), (1, 0)])
    total = swaps(total, "z_hi", 4, (1,), jnp.add)
    total = swaps(total, "z_hi", 4, (3,), jnp.add)
    return values[:, None, :], total / 32


def solution(mesh):
    fine = Mesh(mesh.devices.reshape(4, 4, 2, 2, 4), ("z_hi", "x", "core", "z_lo", "y"))
    turn, line = ("z_hi", "x", "core"), ("z_lo", "y")
    in_specs = (
        P(),
        P(None, turn),
        P(None, turn, None),
        P(None, turn, None, None),
        P(),
        P(None, turn, line, None, None),
        P(None, turn, None, line, None, None, None, None),
        P(line, None, None, None),
    )
    out_specs = (P(None, turn, None), P())
    return jax.shard_map(local, mesh=fine, in_specs=in_specs, out_specs=out_specs, check_vma=False)
```

```python
import functools

import jax
import jax.numpy as jnp
from jax import lax
from jax.experimental import pallas as pl
from jax.experimental.pallas import tpu as pltpu
from jax.sharding import Mesh
from jax.sharding import PartitionSpec as P

CARDS = 52
LANES = 128
F8 = jnp.float8_e4m3fn
F32 = jnp.float32
BF16 = jnp.bfloat16
GROUP = 4
DEPTH = 256
SPLIT = 8
COPIES = 16


def padded(hands):
    return -(-hands // LANES) * LANES


def hand_cards(width):
    hand = lax.broadcasted_iota(jnp.int32, (1, width), 1)

    def first_of(lower):
        return (lower * (2 * CARDS - 1 - lower)) >> 1

    root = jnp.sqrt(jnp.maximum(((2 * CARDS - 1) ** 2 - 8 * hand).astype(F32), 0.0))
    lower = ((2 * CARDS - 1 - root) * 0.5).astype(jnp.int32)
    lower = lower + (first_of(lower + 1) <= hand).astype(jnp.int32)
    lower = lower - (first_of(lower) > hand).astype(jnp.int32)
    return lower, hand - first_of(lower) + lower + 1


def ordered(ranks):
    octave = ranks >> 7
    low = jnp.left_shift(1, jnp.minimum(octave, 29)).astype(F32)
    high = jnp.left_shift(1, jnp.maximum(octave - 29, 0)).astype(F32)
    return ((ranks & 127) + 128).astype(F32) * low * high


def board_kernel(
    flop_cards_in, turn_cards_in, river_cards_in, ranks_in, flop_reach_in, turn_in, stake_in, river_in, out_ref,
    flop_cards, turn_cards, river_cards, ranks_ref, flop_reach_ref, turn_ref, stake_ref, river_ref,
    free_ref, rows_ref, columns_ref, wide_ref, clear_ref, entry_ref, payoff_ref, leaves_ref, sems, river_sems, *, hands,
):
    flops, rivers = river_cards.shape
    boards = flops * rivers
    width = padded(hands)
    depth = -(-hands // 64) * 64
    group = GROUP
    tiles = [(at, min(256, width - at)) for at in range(0, width, 256)]
    pairs = [
        (flop_cards_in, flop_cards), (turn_cards_in, turn_cards), (river_cards_in, river_cards), (ranks_in, ranks_ref),
        (flop_reach_in, flop_reach_ref), (turn_in, turn_ref), (stake_in, stake_ref),
    ]
    copies = [pltpu.make_async_copy(source, target, sems.at[i]) for i, (source, target) in enumerate(pairs)]
    for i in (3, 5, 4, 6, 0, 1, 2):
        copies[i].start()

    def river_copy(board):
        return pltpu.make_async_copy(river_in.at[board], river_ref.at[board], river_sems.at[board])

    for board in range(boards):
        river_copy(board).start()

    lower, upper = hand_cards(width)
    card = lax.broadcasted_iota(jnp.int32, (64, width), 0)
    holds = jnp.where((card == lower) | (card == upper), 1.0, 0.0).astype(BF16)
    for at, size in tiles:
        shared = lax.dot_general(holds, holds[:, at:at + size], (((0,), (0,)), ((), ())), preferred_element_type=F32)
        free = jnp.maximum(1.0 - shared, 0.0).astype(BF16)
        free_ref[:, at:at + size] = free
    copies[3].wait()
    strength = ordered(ranks_ref[...])
    strength = jnp.concatenate([strength, jnp.zeros((boards, width - hands), F32)], axis=1)
    for row in range(boards):
        rows_ref[row] = jnp.broadcast_to(strength[row:row + 1], (16, width)).astype(BF16)
    for at in range(0, width, LANES):
        columns_ref[at:at + LANES, :] = strength[:, at:at + LANES].T.astype(BF16)
    half = SPLIT
    for board in range(half, boards):
        for down in range(0, depth, 64):
            column = columns_ref[down:down + 64, board:board + 1].astype(F32)
            wide_ref[board, down:down + 64, :] = jnp.broadcast_to(column, (64, LANES)).astype(BF16)
    for board in range(0, half, 2):
        lane = lax.broadcasted_iota(jnp.int32, (boards, 2 * LANES), 1) // LANES + board
        pick = (lane == lax.broadcasted_iota(jnp.int32, lane.shape, 0)).astype(BF16)
        both = jnp.dot(columns_ref[:depth, :], pick, preferred_element_type=F32).astype(BF16)
        wide_ref[board, :depth] = both[:, :LANES]
        wide_ref[board + 1, :depth] = both[:, LANES:]

    for i in (0, 1, 2, 4, 5, 6):
        copies[i].wait()

    def clear_of(card):
        return jnp.where((lower == card) | (upper == card), 0.0, 1.0)

    def widen(values):
        return jnp.concatenate([values, jnp.zeros((values.shape[0], width - hands), F32)], axis=1)

    for flop in range(flops):
        clear = clear_of(turn_cards[flop])
        for i in range(3):
            clear = clear * clear_of(flop_cards[flop, i])
        clear_ref[flop] = clear
        turn = turn_ref[flop].astype(F32)
        turn_prob = turn / jnp.sum(turn, axis=0, keepdims=True)
        entry_ref[flop] = widen(flop_reach_ref[flop:flop + 1, :] * turn_prob) * clear

    stake16 = stake_ref[...].reshape(16, 4)
    lane = lax.broadcasted_iota(jnp.int32, (16, 64), 1)
    own = (lane >> 2) == lax.broadcasted_iota(jnp.int32, (16, 64), 0)
    pots = jnp.zeros((16, 64), F32)
    for reply in range(4):
        pots = jnp.where((lane & 3) == reply, stake16[:, reply:reply + 1], pots)
    pots = jnp.where(own, pots, 0.0)
    coarse = pots.astype(BF16)
    spread = jnp.concatenate([own.astype(BF16), coarse, (pots - coarse.astype(F32)).astype(BF16)], axis=0)

    def one_group(at_group, acc):
        first = at_group * group
        flop = first // rivers
        lines, clears = [], []
        for i in range(group):
            river_copy(first + i).wait()
        for i in range(group):
            sums = jnp.dot(spread, river_ref[first + i].reshape(64, hands), preferred_element_type=F32)
            share = (sums[16:32] + sums[32:48]) / sums[:16]
            clear = clear_of(river_cards[flop, lax.rem(first + i, rivers)])
            reach = share.reshape(4, 4, hands) * (entry_ref[flop] * clear)[:, None, :hands]
            lines.append(widen(reach.reshape(16, hands)).astype(BF16))
            clears.append(clear)
        for chunk in range(0, depth, DEPTH):
            stop = min(chunk + DEPTH, depth)
            for down in range(chunk, stop, 32):
                column = [wide_ref[first + i, down:down + 32, :] for i in range(group)]
                for at in range(0, width, LANES):
                    free = free_ref[down:down + 32, at:at + LANES]
                    for i in range(group):
                        row = rows_ref[first + i, :, at:at + LANES]
                        gap = jnp.concatenate([row, row], axis=0) - column[i]
                        sign = jnp.minimum(jnp.maximum(gap, -1.0), 1.0) * free
                        payoff_ref[i, down:down + 32, at:at + LANES] = sign.astype(F8)
            for i in range(group):
                product = jnp.dot(lines[i][:, chunk:stop], payoff_ref[i, chunk:stop, :], preferred_element_type=F32)
                if chunk == 0:
                    leaves_ref[i] = product
                else:
                    leaves_ref[i] += product
        value = jnp.zeros((1, width), F32)
        for i in range(group):
            best = jnp.max(leaves_ref[i].reshape(4, 4, width), axis=1)
            value = value + jnp.sum(best, axis=0, keepdims=True) * clears[i]
        return acc + value

    groups = rivers // group
    for flop in range(flops):
        value = lax.fori_loop(flop * groups, (flop + 1) * groups, one_group, jnp.zeros((1, width), F32))
        result = (value * clear_ref[flop] * (1 / rivers))[:, :hands]
        for i in range(out_ref.shape[0]):
            out_ref[i, flop:flop + 1, :] = result


def board_values(flop_cards, turn_cards, river_cards, ranks, flop_reach, turn_policy, river_policy, stake):
    flops, rivers, hands = ranks.shape
    boards = flops * rivers
    width = padded(hands)
    args = (
        flop_cards, turn_cards, river_cards, ranks.reshape(boards, hands), flop_reach, turn_policy, stake,
        river_policy.reshape(boards, 16, 4, hands),
    )
    held = [(pltpu.SMEM if i < 3 else pltpu.VMEM)(a.shape, a.dtype) for i, a in enumerate(args)]
    return pl.pallas_call(
        functools.partial(board_kernel, hands=hands),
        in_specs=[pl.BlockSpec(memory_space=pl.ANY)] * len(args),
        out_specs=pl.BlockSpec(memory_space=pltpu.VMEM),
        out_shape=pltpu.VMEM((COPIES, flops, hands), F32),
        scratch_shapes=held + [
            pltpu.VMEM((width, width), BF16),
            pltpu.VMEM((boards, 16, width), BF16),
            pltpu.VMEM((width, boards), BF16),
            pltpu.VMEM((boards, width, LANES), BF16),
            pltpu.VMEM((flops, 1, width), F32),
            pltpu.VMEM((flops, 4, width), F32),
            pltpu.VMEM((GROUP, width, width), F8),
            pltpu.VMEM((GROUP, 16, width), F32),
            pltpu.SemaphoreType.DMA((len(args) - 1,)),
            pltpu.SemaphoreType.DMA((boards,)),
        ],
        compiler_params=pltpu.CompilerParams(vmem_limit_bytes=56 * 2**20),
        name="boards",
    )(*args)


def swaps(values, axis, size, flips, combine):
    parts = [lax.ppermute(values, axis, [(i, i ^ flip) for i in range(size)]) for flip in flips]
    return functools.reduce(combine, parts, values)


def local(flop_cards, turn_cards, river_cards, ranks, flop_reach, turn_policy, river_policy, stake):
    copies = board_values(
        flop_cards, turn_cards[:, 0], river_cards[:, 0], ranks[:, 0], flop_reach, turn_policy[:, 0, 0],
        river_policy[:, 0, :, 0], stake[0]
    )
    group = ("core", "z_lo", "y")
    gathered = lax.all_to_all(copies, group, 0, 0).reshape(2, -1, *copies.shape[1:])
    first, second = jnp.max(gathered[0], axis=0), jnp.max(gathered[1], axis=0)
    values = jnp.where(lax.axis_index("core") == 0, first, second)
    total = first + second
    pairs = [(2 * i + core, 2 * (i ^ flip) + core) for i in range(4) for core, flip in ((0, 1), (1, 3))]
    near = lax.ppermute(total, ("x", "core"), pairs)
    total = swaps(total, "x", 4, (2,), jnp.add) + near + lax.ppermute(near, "core", [(0, 1), (1, 0)])
    total = swaps(total, "z_hi", 4, (1,), jnp.add)
    total = swaps(total, "z_hi", 4, (3,), jnp.add)
    return values[:, None, :], total / 32


def solution(mesh):
    fine = Mesh(mesh.devices.reshape(4, 4, 2, 2, 4), ("z_hi", "x", "core", "z_lo", "y"))
    turn, line = ("z_hi", "x", "core"), ("z_lo", "y")
    in_specs = (
        P(),
        P(None, turn),
        P(None, turn, None),
        P(None, turn, None, None),
        P(),
        P(None, turn, line, None, None),
        P(None, turn, None, line, None, None, None, None),
        P(line, None, None, None),
    )
    out_specs = (P(None, turn, None), P())
    return jax.shard_map(local, mesh=fine, in_specs=in_specs, out_specs=out_specs, check_vma=False)
```
